256 devices in a mesh: grp: 8 (over z_hi, x), shard: 32 (over y, z_lo, core).
Axes of the slice: x: 4, y: 4, z: 8 (z_hi: 2, z_lo: 4; z = z_hi * 4 + z_lo), core: 2. Of those that a mesh axis runs over, the one named last changes fastest.
Arguments:
- tokens: bfloat16 [131072, 8192], P(('grp', 'shard')), may hold values from -24 to 24
- norm_gain: float32 [8192], replicated, may hold values from 0.1 to 1.9
- codes: int32 [8192, 512], P('shard'), may hold values from 0 to 15
- zero_points: int32 [64, 512], P('shard'), may hold values from 0 to 15
- scales: float32 [64, 512], P('shard'), may hold values from 0.0008 to 0.008
- key_grad: bfloat16 [131072, 512], P(('grp', 'shard')), may hold values from -0.016479492 to 0.016479492
Outputs:
- keys: bfloat16 [131072, 512], P(('grp', 'shard'))
- weight_grad: float32 [8192, 512], P('shard')
The draws below stay inside these ranges and needn't reach their ends.
All inputs are finite; a program needn't handle non-finite values.
Results may differ from the reference program's by a relative error of at most 0.0058.
Values may be sent and summed in bfloat16 or wider, within the bound.
A program may use at most 128 MiB of HBM per device.

```python
import math
import jax
import jax.numpy as jnp
from jax import lax

D = 8192
KV = 512
GROUP = 128
TOK_DEV = 512
TOKENS = 131072


def touch_ends(array, rng, low, largest):
    extent = array.shape
    place = [jax.random.randint(jax.random.fold_in(rng, axis), (), 0, extent[axis]) for axis in range(len(extent))]
    array = array.at[tuple(place)].set(low)
    longest = extent.index(max(extent))
    place[longest] = (place[longest] + 1) % extent[longest]
    return array.at[tuple(place)].set(largest)


def spiked(values, rng, source, target, parts, factor):
    def block_of(position):
        return (jnp.arange(values.shape[position]) // (values.shape[position] // parts)).reshape((-1,) + (1,) * (values.ndim - 1 - position))

    near = jax.random.permutation(rng, parts)[block_of(target)]
    far = (block_of(target) + parts // 2) % parts
    return jnp.where((block_of(source) == near) | (block_of(source) == far), factor * values, values)


def level_of(rng, extent, split, least, top_value):
    factor_of, own = 1.0, jax.random.fold_in(rng, 6)
    for axis_at, blocks in split:
        draws = jnp.exp(jax.random.uniform(jax.random.fold_in(own, axis_at), (blocks,), jnp.float32, least / len(split), top_value / len(split)))
        factor_of = factor_of * jnp.repeat(draws, extent[axis_at] // blocks).reshape([-1 if axis == axis_at else 1 for axis in range(len(extent))])
    return factor_of


def noise(key, shape, deviation, bound, cuts=(), held_as=jnp.bfloat16):
    loudness = level_of(key, shape, cuts, -0.22, 0.18) if cuts else 1.0
    array = jax.random.normal(key, shape, jnp.float32) * deviation * loudness
    return jnp.minimum(jnp.maximum(array, -bound), bound).astype(held_as)


def noise_with(key, extent, scale, limit, pieces, heavy, dtype=jnp.bfloat16):
    values = scale * jax.random.normal(key, extent, jnp.float32)
    if pieces:
        values = values * level_of(key, extent, pieces, -0.22, 0.18)
    return jnp.clip(spiked(values, jax.random.fold_in(key, 3), *heavy), -limit, limit).astype(dtype)


def setup_inputs(seed: int = 0) -> dict:
    arg_keys = jax.random.split(jax.random.key(seed), 7)
    return {
        "tokens": noise_with(arg_keys[0], (TOKENS, D), 1.0, 24.0, ((0, 256),), (0, 1, 256, 6.0)),
        "norm_gain": jnp.clip(1.0 + 0.18 * jax.random.normal(arg_keys[1], (D,), jnp.float32), 0.1, 1.9),
        "codes": touch_ends(jax.random.randint(arg_keys[2], (D, KV), 0, 16), jax.random.fold_in(arg_keys[2], 1), 0, 15).astype(jnp.int32),
        "zero_points": touch_ends(jax.random.randint(arg_keys[3], (D // GROUP, KV), 0, 16), jax.random.fold_in(arg_keys[3], 1), 0, 15).astype(jnp.int32),
        "scales": jnp.clip(jnp.exp(math.log(0.008) - 2.3025852 * jax.random.uniform(arg_keys[4], (D // GROUP, KV), jnp.float32) ** level_of(arg_keys[4], (D // GROUP, KV), ((0, 32),), -0.2, 0.2)), 0.0008, 0.008),
        "key_grad": noise(arg_keys[5], (TOKENS, KV), (TOKENS ** -0.5), 0.016479492, ((0, 256),)),
    }


EPS = 1e-05

def dequantize(codes, zero_points, scales):
    shaped = codes.reshape(D // GROUP, GROUP, KV) - zero_points[:, None, :]
    weight = shaped.astype(jnp.float32) * scales[:, None, :]
    return weight.astype(jnp.bfloat16).reshape(D, KV)

def reference(tokens, norm_gain, codes, zero_points, scales, key_grad):
    weight = dequantize(codes, zero_points, scales)
    token_blocks = tokens.reshape(-1, TOK_DEV, D)
    grad_blocks = key_grad.reshape(-1, TOK_DEV, KV)

    def one_block(total, inputs):
        block, grads = inputs
        values = block.astype(jnp.float32)
        mean_sq = lax.optimization_barrier(jnp.mean(values * values, axis=-1, keepdims=True))
        normed = (values * lax.rsqrt(mean_sq + EPS) * norm_gain.astype(jnp.float32)).astype(jnp.bfloat16)
        keys = jnp.dot(normed, weight, preferred_element_type=jnp.float32).astype(jnp.bfloat16)
        term = lax.dot_general(normed, grads, (((0,), (0,)), ((), ())), preferred_element_type=jnp.float32)
        return (total + term, keys)
    start = jnp.zeros((D, KV), jnp.float32)
    weight_grad, keys = lax.scan(one_block, start, (token_blocks, grad_blocks))
    return (keys.reshape(-1, KV), weight_grad)
```

```python
import jax
import jax.numpy as jnp
from jax import lax
from jax.experimental import pallas as pl
from jax.experimental.pallas import tpu as pltpu
from jax.sharding import PartitionSpec as P

EPS = 1e-05
D, KV, TOK = 8192, 512, 512
BLK = 256
MESH = pl.DeviceIdType.MESH
BF, F32 = jnp.bfloat16, jnp.float32
ORDER = (0, 1, 3, 2)
BLOCKS = [(0, 0), (0, 1), (0, 3), (1, 0), (3, 0), (0, 2), (2, 0), (1, 1), (1, 3), (3, 1), (3, 3), (1, 2), (3, 2), (2, 1), (2, 3), (2, 2)]
NCH = 16
LAG2, LAGF = 2, 4
SLOT_A, SLOT_B, SLOT_C, SLOT_D = 1, 3, 8, 10
KEYS0 = 3
NT = 8


def gray(i):
    return i + (i // 2) * (1 - 2 * (i % 2))


def pick(table, m):
    value = table[0]
    for n in range(1, len(table)):
        value = jnp.where(m == n, table[n], value)
    return value


def kernel(tok_h, gain_h, codes_h, zp_h, sc_h, kg_h, keys_ref, grad_ref,
           t, w, gain, codes, zp, sc, kg, kt, rkt, rcol, own, psend, prec, comb, xt, xs, xf, ys, ysum, yr, zs, zr, fin, acc,
           lsem, s_p, r_p, s_xt, r_xt, s_xf, r_xf, s_y, r_y, s_z, r_z, s_f, r_f, s_ag, r_ag, s_w, r_w):
    g, s = lax.axis_index("grp"), lax.axis_index("shard")
    x, zh = lax.rem(g, 4), lax.div(g, 4)
    y, zl, c = lax.div(s, 8), lax.rem(lax.div(s, 2), 4), lax.rem(s, 2)
    z = zh * 4 + zl

    def at(ax, ay, az, ac):
        ax, ay, az = lax.rem(ax, 4), lax.rem(ay, 4), lax.rem(az, 8)
        return (lax.div(az, 4) * 4 + ax, (ay * 4 + lax.rem(az, 4)) * 2 + ac)

    partner = at(x, y, z, 1 - c)
    xl, xr = at(x + 3, y, z, c), at(x + 1, y, z, c)
    hop = {("y", 0): at(x, y + 1, z, c), ("y", 1): at(x, y + 3, z, c), ("z", 0): at(x, y, z + 1, c), ("z", 1): at(x, y, z + 7, c)}

    def block(dy, dz, core):
        return (lax.rem(y + dy, 4) * 4 + lax.rem(zl + dz, 4)) * 2 + core

    def send(src, dst, ss, rs, to):
        return pltpu.make_async_remote_copy(src_ref=src, dst_ref=dst, send_sem=ss, recv_sem=rs, device_id=to, device_id_type=MESH)

    loads = [pltpu.make_async_copy(a, b, lsem.at[i]) for i, (a, b) in enumerate(
        [(codes_h, codes), (zp_h, zp), (sc_h, sc), (gain_h, gain), (kg_h, kg)])]
    for cp in loads:
        cp.start()
    rows_t = TOK // NT

    def load_t(i):
        r = pl.ds(pl.multiple_of(i * rows_t, rows_t), rows_t)
        return pltpu.make_async_copy(tok_h.at[r], t.at[r], lsem.at[5 + i])

    for i in range(NT):
        load_t(i).start()

    barrier = pltpu.get_barrier_semaphore()
    peers = [partner] + [at(x + i, y, z, c) for i in (1, 2, 3)] + [at(x, y + i, z, c) for i in (1, 2, 3)]
    peers += [at(x, y, z + i, c) for i in range(1, 8)]
    for p in peers:
        pl.semaphore_signal(barrier, inc=1, device_id=p, device_id_type=MESH)

    for cp in loads[:4]:
        cp.wait()
    mine = block(0, 0, c)
    for j in range(2):
        row = gain[pl.ds(2 * s + j, 1), :]
        col = jnp.transpose(jnp.broadcast_to(row, (128, 128)))
        part = pl.ds(j * 128, 128)
        for q in range(4):
            lanes = pl.ds(q * 128, 128)
            shaped = (codes[part, lanes] - zp[pl.ds(j, 1), lanes]).astype(F32)
            w[mine, part, lanes] = (shaped * sc[pl.ds(j, 1), lanes] * col).astype(BF)

    pl.semaphore_wait(barrier, len(peers))

    def ag(h, n, way, kind):
        axis = ("y", "z")[(h + (n > 0)) % 2]
        dp = ORDER[n - 1] if n > 0 else 0
        off = 0 if kind == 0 else (3, 1)[way]
        if n == 0:
            dp, dq = off, 0
        else:
            dq = off
        dy, dz = (dp, dq) if h == 0 else (dq, dp)
        lo, size = (h * 128, 128) if kind == 0 else (h * 128 + 64 * way, 64)
        ref = w.at[block(dy, dz, c), pl.ds(lo, size)]
        i = ((h * 5 + n) * 2 + way) * 2 + kind
        return send(ref, ref, s_ag.at[i], r_ag.at[i], hop[(axis, way)])

    def ag_start(n, kind):
        for h in range(2):
            for way in range(2):
                ag(h, n, way, kind).start()

    def ag_wait(n, kind):
        for h in range(2):
            for way in range(2):
                ag(h, n, way, kind).wait_recv()

    def share(m):
        dy, dz = BLOCKS[m]
        ref = w.at[block(dy, dz, c)]
        return send(ref, ref, s_w.at[m], r_w.at[m], partner)

    ag_start(0, 0)
    ag_start(1, 0)
    share(0).start()

    loads[4].wait()
    kt[...] = jnp.transpose(kg[...].astype(F32))

    def norm_rows(i, carry):
        load_t(i).wait()

        def tile(u, carry):
            r0 = pl.multiple_of(i * rows_t + u * 16, 16)
            sums = [jnp.zeros((16, 128), F32) for _ in range(4)]
            for v in range(D // 128):
                val = t[pl.ds(r0, 16), pl.ds(v * 128, 128)].astype(F32)
                sums[v % 4] = sums[v % 4] + val * val
            total = jnp.sum((sums[0] + sums[1]) + (sums[2] + sums[3]), axis=1, keepdims=True)
            rcol[pl.ds(r0, 16), :] = jnp.broadcast_to(lax.rsqrt(total * (1.0 / D) + EPS), (16, 128))
            return carry

        return lax.fori_loop(0, rows_t // 16, tile, carry)

    lax.fori_loop(0, NT, norm_rows, 0)
    for q in range(4):
        lanes = pl.ds(q * 128, 128)
        row = jnp.transpose(rcol[lanes, :])[0:1, :]
        rkt[:, lanes] = (kt[:, lanes] * row).astype(BF)

    def place(k):
        return gray(3 - k % 4), gray(k // 4)

    def term(b):
        cols = pl.ds(pl.multiple_of(b * BLK, BLK), BLK)
        return jnp.dot(rkt[...], t[:, cols], preferred_element_type=F32)

    def to_partner(k):
        return send(psend.at[k], prec.at[k], s_p.at[k], r_p.at[k], partner)

    def piece(dx, half):
        return pl.ds(pl.multiple_of(lax.rem(x + dx, 4) * 128 + half * 64, 64), 64)

    def x_first(k):
        return [
            send(comb.at[k, piece(2, 0)], xt.at[0, k], s_xt.at[0, k], r_xt.at[0, k], xl),
            send(comb.at[k, piece(2, 1)], xt.at[1, k], s_xt.at[1, k], r_xt.at[1, k], xr),
            send(comb.at[k, piece(1, 0)], xf.at[0, k], s_xf.at[0, k], r_xf.at[0, k], xr),
            send(comb.at[k, piece(3, 1)], xf.at[1, k], s_xf.at[1, k], r_xf.at[1, k], xl),
        ]

    def x_second(k):
        return [
            send(xs.at[0, k], xf.at[2, k], s_xf.at[2, k], r_xf.at[2, k], xl),
            send(xs.at[1, k], xf.at[3, k], s_xf.at[3, k], r_xf.at[3, k], xr),
        ]

    def to_y(k):
        dy, _ = place(k)
        n = (k // 4) * 3 + k % 4
        return send(ys.at[k], yr.at[n], s_y.at[n], r_y.at[n], at(x, y + dy, z, c))

    def to_z(j, way):
        to = at(x, y, z + gray(j) + 4 * way, c)
        return send(zs.at[j], zr.at[z], s_z.at[j, way], r_z.at[z], to)

    def gradient(k):
        dy, dz = place(k)
        psend[k] = term(block(dy, dz, 1 - c)).astype(BF)
        to_partner(k).start()
        own[k % 2] = term(block(dy, dz, c))

    def combine(k):
        to_partner(k).wait_recv()
        comb[k] = (own[k % 2] + prec[k].astype(F32)).astype(BF)
        for cp in x_first(k):
            cp.start()

    def second(k):
        first = x_first(k)
        later = x_second(k)
        for i, dx in ((0, 3), (1, 1)):
            first[i].wait_recv()
            xs[i, k] = (comb[k, piece(dx, i), :].astype(F32) + xt[i, k].astype(F32)).astype(BF)
            later[i].start()

    def final(k):
        first = x_first(k)
        later = x_second(k)
        for cp in (first[2], first[3], later[0], later[1]):
            cp.wait_recv()
        a = comb[k, piece(0, 0), :].astype(F32) + xf[0, k].astype(F32) + xf[2, k].astype(F32)
        b = comb[k, piece(0, 1), :].astype(F32) + xf[1, k].astype(F32) + xf[3, k].astype(F32)

        @pl.when(k % 4 != 3)
        def _():
            ys[k, pl.ds(0, 64), :] = a.astype(BF)
            ys[k, pl.ds(64, 64), :] = b.astype(BF)
            to_y(k).start()

        @pl.when(k % 4 == 3)
        def _():
            ysum[pl.ds(0, 64), :] = a
            ysum[pl.ds(64, 64), :] = b
            j = k // 4
            for i in range(3):
                to_y(j * 4 + i).wait_recv()
            total = ysum[...]
            for i in range(3):
                total = total + yr[j * 3 + i].astype(F32)
            zs[j] = total.astype(BF)

            @pl.when(j == 0)
            def _():
                zr[z] = total.astype(BF)

            @pl.when(j != 0)
            def _():
                to_z(j, 0).start()

            to_z(j, 1).start()

    def sent(k):
        for cp in [to_partner(k)] + x_first(k) + x_second(k):
            cp.wait_send()

        @pl.when(k % 4 != 3)
        def _():
            to_y(k).wait_send()

    def keys_step(m):
        dy, dz = pick([b[0] for b in BLOCKS], m), pick([b[1] for b in BLOCKS], m)
        ref = w.at[block(dy, dz, 1 - c)]
        send(ref, ref, s_w.at[m], r_w.at[m], partner).wait_recv()
        for core in range(2):
            b = block(dy, dz, core)
            cols = pl.ds(pl.multiple_of(b * BLK, BLK), BLK)
            acc[...] += jnp.dot(t[:, cols], w[b], preferred_element_type=F32)

    acc[...] = jnp.zeros_like(acc)

    def step(k, carry):
        @pl.when(k < NCH)
        def _():
            gradient(k)

        @pl.when(jnp.logical_and(k >= 1, k < NCH + 1))
        def _():
            combine(k - 1)

        @pl.when(k == SLOT_A)
        def _():
            ag_wait(0, 0)
            ag_start(0, 1)
            ag_start(2, 0)
            ag_start(3, 0)
            ag_wait(1, 0)
            ag_start(1, 1)
            for m in range(1, 5):
                share(m).start()

        @pl.when(k == SLOT_B)
        def _():
            ag_wait(0, 1)
            ag_start(4, 0)
            for n in (2, 3):
                ag_wait(n, 0)
                ag_start(n, 1)
            ag_wait(1, 1)
            for m in range(5, 11):
                share(m).start()

        @pl.when(k == SLOT_C)
        def _():
            ag_wait(4, 0)
            ag_start(4, 1)
            ag_wait(2, 1)
            ag_wait(3, 1)
            for m in range(11, 15):
                share(m).start()

        @pl.when(k == SLOT_D)
        def _():
            ag_wait(4, 1)
            share(15).start()

        @pl.when(jnp.logical_and(k >= 1 + LAG2, k < NCH + 1 + LAG2))
        def _():
            second(k - 1 - LAG2)

        @pl.when(jnp.logical_and(k >= 1 + LAGF, k < NCH + 1 + LAGF))
        def _():
            final(k - 1 - LAGF)

        @pl.when(jnp.logical_and(k >= KEYS0, k < KEYS0 + NCH))
        def _():
            keys_step(k - KEYS0)

        return carry

    lax.fori_loop(0, NCH + 1 + LAGF, step, 0)

    for q in range(4):
        lanes = pl.ds(q * 128, 128)
        keys_ref[:, lanes] = (acc[:, lanes] * rcol[...]).astype(BF)

    def waits(k, carry):
        sent(k)
        return carry

    lax.fori_loop(0, NCH, waits, 0)
    for h in range(2):
        for n in range(5):
            for way in range(2):
                for kind in range(2):
                    ag(h, n, way, kind).wait_send()
    for m in range(16):
        share(m).wait_send()
    for j in range(4):
        for way in range(2):
            if j or way:
                to_z(j, way).wait_send()

    for i in range(1, 8):
        src = lax.rem(z + i, 8)
        send(zs.at[0], zr.at[src], s_z.at[0, 0], r_z.at[src], partner).wait_recv()
    total = zr[0].astype(F32)
    for i in range(1, 8):
        total = total + zr[i].astype(F32)
    fin[x] = total.astype(BF)

    outs = [send(fin.at[x], fin.at[x], s_f.at[i - 1], r_f.at[x], at(x + i, y, z, c)) for i in (1, 3, 2)]
    for cp in outs:
        cp.start()
    for i in range(1, 4):
        src = lax.rem(x + i, 4)
        send(fin.at[src], fin.at[src], s_f.at[0], r_f.at[src], xl).wait_recv()
    row = jnp.concatenate([gain[pl.ds(2 * s, 1), :], gain[pl.ds(2 * s + 1, 1), :]], axis=1)
    for q in range(4):
        grad_ref[:, pl.ds(q * 128, 128)] = jnp.transpose(fin[q].astype(F32) * row)
    for cp in outs:
        cp.wait_send()


def per_device(tokens, norm_gain, codes, zero_points, scales, key_grad):
    hbm = pl.BlockSpec(memory_space=pl.ANY)
    vmem = pl.BlockSpec(memory_space=pltpu.VMEM)
    sem = pltpu.SemaphoreType.DMA
    v = pltpu.VMEM
    return pl.pallas_call(
        kernel,
        out_shape=(jax.ShapeDtypeStruct((TOK, KV), BF), jax.ShapeDtypeStruct((BLK, KV), F32)),
        in_specs=[hbm] * 6,
        out_specs=(vmem, vmem),
        scratch_shapes=[
            v((TOK, D), BF), v((32, BLK, KV), BF), v((64, 128), F32), v((BLK, KV), jnp.int32), v((2, KV), jnp.int32),
            v((2, KV), F32), v((TOK, KV), BF), v((KV, TOK), F32), v((KV, TOK), BF), v((TOK, 128), F32),
            v((2, KV, BLK), F32), v((NCH, KV, BLK), BF), v((NCH, KV, BLK), BF), v((NCH, KV, BLK), BF),
            v((2, NCH, 64, BLK), BF), v((2, NCH, 64, BLK), BF), v((4, NCH, 64, BLK), BF),
            v((NCH, 128, BLK), BF), v((128, BLK), F32), v((12, 128, BLK), BF), v((4, 128, BLK), BF), v((8, 128, BLK), BF),
            v((4, 128, BLK), BF), v((TOK, KV), F32),
            sem((5 + NT,)), sem((NCH,)), sem((NCH,)), sem((2, NCH)), sem((2, NCH)), sem((4, NCH)), sem((4, NCH)),
            sem((12,)), sem((12,)), sem((4, 2)), sem((8,)), sem((3,)), sem((4,)), sem((40,)), sem((40,)), sem((16,)), sem((16,)),
        ],
        compiler_params=pltpu.CompilerParams(collective_id=1, has_side_effects=True, vmem_limit_bytes=56 * 2**20),
        cost_estimate=pl.CostEstimate(flops=8 * TOK * D * KV // 2, bytes_accessed=12 * 2**20, transcendentals=TOK),
        name="layer",
    )(tokens, norm_gain.reshape(64, 128), codes, zero_points, scales, key_grad)


def solution(mesh):
    in_specs = (
        P(("grp", "shard"), None),
        P(),
        P("shard", None),
        P("shard", None),
        P("shard", None),
        P(("grp", "shard"), None),
    )
    out_specs = (P(("grp", "shard"), None), P("shard", None))
    return jax.shard_map(
        per_device, mesh=mesh, in_specs=in_specs, out_specs=out_specs, check_vma=False
    )
```

```python
import jax
import jax.numpy as jnp
from jax import lax
from jax.experimental import pallas as pl
from jax.experimental.pallas import tpu as pltpu
from jax.sharding import PartitionSpec as P

EPS = 1e-05
D, KV, TOK = 8192, 512, 512
BLK = 256
MESH = pl.DeviceIdType.MESH
BF, F32 = jnp.bfloat16, jnp.float32
ORDER = (0, 1, 3, 2)
PIECES = ((2, 0), (3, 1), (2, 1), (1, 0), (3, 0), (1, 1), (0, 0), (0, 1))
BLOCKS = [(0, 0), (0, 1), (0, 3), (1, 0), (3, 0), (0, 2), (2, 0), (1, 1), (1, 3), (3, 1), (3, 3), (1, 2), (3, 2), (2, 1), (2, 3), (2, 2)]
NCH = 13
YPOS = 11
YSEC = 6
CUT = 192
LAG2 = 2
LAGF = 5
LAGS = 8
SLOT_A = 1
SLOT_B = 7
SLOT_C = 12
SLOT_B0 = 5
KEYS0 = 9
NT = 16
FLY = 6


def gray(i):
    return i + (i // 2) * (1 - 2 * (i % 2))


def pick(table, m):
    value = table[0]
    for n in range(1, len(table)):
        value = jnp.where(m == n, table[n], value)
    return value


def kernel(tok_h, gain_h, codes_h, zp_h, sc_h, kg_h, keys_h, fin_h,
           t, w, gain, codes, zp, sc, kg, kt, rkt, rcol, own, psend, prec, comb, xt, xs, xf, ys, ysum, yr, zs, zr, fin, acc, keys_ref,
           yc, yt, yd, yu, ye, s_yy, r_yy,
           lsem, s_l, r_l, s_p, r_p, s_xt, r_xt, s_xf, r_xf, s_y, r_y, s_z, r_z, s_f, r_f, s_ag, r_ag, s_w, r_w):
    g, s = lax.axis_index("grp"), lax.axis_index("shard")
    x, zh = lax.rem(g, 4), lax.div(g, 4)
    y, zl, c = lax.div(s, 8), lax.rem(lax.div(s, 2), 4), lax.rem(s, 2)
    z = zh * 4 + zl

    def at(ax, ay, az, ac):
        ax, ay, az = lax.rem(ax, 4), lax.rem(ay, 4), lax.rem(az, 8)
        return (lax.div(az, 4) * 4 + ax, (ay * 4 + lax.rem(az, 4)) * 2 + ac)

    partner = at(x, y, z, 1 - c)
    xl, xr = at(x + 3, y, z, c), at(x + 1, y, z, c)
    hop = {("y", 0): at(x, y + 1, z, c), ("y", 1): at(x, y + 3, z, c), ("z", 0): at(x, y, z + 1, c), ("z", 1): at(x, y, z + 7, c)}

    def block(dy, dz, core):
        return (lax.rem(y + dy, 4) * 4 + lax.rem(zl + dz, 4)) * 2 + core

    def send(src, dst, ss, rs, to):
        return pltpu.make_async_remote_copy(src_ref=src, dst_ref=dst, send_sem=ss, recv_sem=rs, device_id=to, device_id_type=MESH)

    barrier = pltpu.get_barrier_semaphore()
    peers = [partner] + [at(x + i, y, z, c) for i in (1, 2, 3)] + [at(x, y + i, z, c) for i in (1, 2, 3)]
    peers += [at(x, y, z + i, c) for i in range(1, 8)]
    for p in peers:
        pl.semaphore_signal(barrier, inc=1, device_id=p, device_id_type=MESH)

    loads = [pltpu.make_async_copy(a, b, lsem.at[i]) for i, (a, b) in enumerate(
        [(codes_h, codes), (zp_h, zp), (sc_h, sc), (gain_h, gain), (kg_h, kg)])]
    for cp in loads:
        cp.start()
    rows_t = TOK // NT

    def load_t(i):
        r = pl.ds(pl.multiple_of(i * rows_t, rows_t), rows_t)
        return pltpu.make_async_copy(tok_h.at[r], t.at[r], lsem.at[5 + i])

    for i in range(FLY):
        load_t(i).start()

    for cp in loads[:4]:
        cp.wait()
    mine = block(0, 0, c)
    for j in range(2):
        row = gain[pl.ds(2 * s + j, 1), :]
        col = jnp.transpose(jnp.broadcast_to(row, (128, 128)))
        part = pl.ds(j * 128, 128)
        for q in range(4):
            lanes = pl.ds(q * 128, 128)
            shaped = (codes[part, lanes] - zp[pl.ds(j, 1), lanes]).astype(F32)
            w[mine, part, lanes] = (shaped * sc[pl.ds(j, 1), lanes] * col).astype(BF)

    pl.semaphore_wait(barrier, len(peers))

    def ag(h, n, way, kind):
        axis = ("y", "z")[(h + (n > 0)) % 2]
        dp = ORDER[n - 1] if n > 0 else 0
        off = 0 if kind == 0 else (3, 1)[way]
        if n == 0:
            dp, dq = off, 0
        else:
            dq = off
        dy, dz = (dp, dq) if h == 0 else (dq, dp)
        size = (CUT, BLK - CUT)[h]
        lo = h * CUT
        if kind == 1:
            size = size // 2
            lo = lo + size * way
        ref = w.at[block(dy, dz, c), pl.ds(lo, size)]
        i = ((h * 5 + n) * 2 + way) * 2 + kind
        return send(ref, ref, s_ag.at[i], r_ag.at[i], hop[(axis, way)])

    def ag_start(n, kind):
        for h in range(2):
            for way in range(2):
                ag(h, n, way, kind).start()

    def ag_wait(n, kind):
        for h in range(2):
            for way in range(2):
                ag(h, n, way, kind).wait_recv()

    def share(m):
        dy, dz = BLOCKS[m]
        ref = w.at[block(dy, dz, c)]
        return send(ref, ref, s_w.at[m], r_w.at[m], partner)

    ag_start(0, 0)
    ag_start(1, 0)
    share(0).start()

    loads[4].wait()
    kt[...] = jnp.transpose(kg[...].astype(F32))

    def norm_rows(i, carry):
        load_t(i).wait()

        @pl.when(i + FLY < NT)
        def _():
            load_t(i + FLY).start()

        def tile(u, carry):
            r0 = pl.multiple_of(i * rows_t + u * 16, 16)
            sums = [jnp.zeros((16, 128), F32) for _ in range(4)]
            for v in range(D // 128):
                val = t[pl.ds(r0, 16), pl.ds(v * 128, 128)].astype(F32)
                sums[v % 4] = sums[v % 4] + val * val
            total = jnp.sum((sums[0] + sums[1]) + (sums[2] + sums[3]), axis=1, keepdims=True)
            rcol[pl.ds(r0, 16), :] = jnp.broadcast_to(lax.rsqrt(total * (1.0 / D) + EPS), (16, 128))
            return carry

        return lax.fori_loop(0, rows_t // 16, tile, carry)

    lax.fori_loop(0, NT, norm_rows, 0)
    for q in range(4):
        lanes = pl.ds(q * 128, 128)
        row = jnp.transpose(rcol[lanes, :])[0:1, :]
        for i, (dx, half) in enumerate(PIECES):
            src = pl.ds(pl.multiple_of(lax.rem(x + dx, 4) * 128 + half * 64, 64), 64)
            rkt[pl.ds(i * 64, 64), lanes] = (kt[src, lanes] * row).astype(BF)

    def place(k):
        e = k - (k > YPOS).astype(jnp.int32)
        return e // 4, e % 4

    def term(b):
        cols = pl.ds(pl.multiple_of(b * BLK, BLK), BLK)
        return jnp.dot(rkt[...], t[:, cols], preferred_element_type=F32)

    def to_partner(n):
        return send(psend.at[n], prec.at[n], s_p.at[n], r_p.at[n], partner)

    def part(i):
        return pl.ds(64 * i, 64)

    def x_first(k):
        return [
            send(comb.at[k, pl.ds(0, 128)], xt.at[1, k], s_xt.at[1, k], r_xt.at[1, k], xl),
            send(comb.at[k, pl.ds(128, 128)], xt.at[0, k], s_xt.at[0, k], r_xt.at[0, k], xr),
        ]

    def x_second(k):
        return [
            send(xs.at[0, k], xf.at[0, k], s_xf.at[0, k], r_xf.at[0, k], xl),
            send(xs.at[1, k], xf.at[1, k], s_xf.at[1, k], r_xf.at[1, k], xr),
        ]

    def to_y(jj, i):
        n = jj * 3 + i
        return send(ys.at[n], yr.at[n], s_y.at[n], r_y.at[n], at(x, y + gray(3 - i), z, c))

    def to_z(j, way):
        to = at(x, y, z + gray(j) + 4 * way, c)
        return send(zs.at[j], zr.at[z], s_z.at[j, way], r_z.at[z], to)

    def last_z(way, half):
        rows = part(half)
        return send(zs.at[3, rows], zr.at[z, rows], s_l.at[way, half], r_l.at[way, half], at(x, y, z + 2 + 4 * way, c))

    def to_x(i, half):
        rows = part(half)
        return send(fin.at[rows], fin_h.at[x, rows], s_f.at[i - 1, half], r_f.at[x, half], at(x + i, y, z, c))

    def gradient(n, dy, dz, held):
        psend[n] = term(block(dy, dz, 1 - c)).astype(BF)
        to_partner(n).start()
        own[held] = term(block(dy, dz, c))

    def both(n, held):
        to_partner(n).wait_recv()
        return (own[held] + prec[n].astype(F32)).astype(BF)

    upper, lower = pl.ds(0, 256), pl.ds(256, 256)

    def y_pass(i):
        src, dst, way = (
            (yc.at[0, upper], yt.at[0], 1),
            (yc.at[0, lower], yt.at[1], 0),
            (yc.at[2, upper], yd.at[0], 0),
            (yc.at[1, lower], yd.at[1], 1),
            (yu.at[0], ye.at[0], 1),
            (yu.at[1], ye.at[1], 0),
        )[i]
        return send(src, dst, s_yy.at[i], r_yy.at[i], hop[("y", way)])

    def y_second():
        y_pass(0).wait_recv()
        yu[0] = (yc[1, upper, :].astype(F32) + yt[0].astype(F32)).astype(BF)
        y_pass(4).start()
        y_pass(1).wait_recv()
        yu[1] = (yc[2, lower, :].astype(F32) + yt[1].astype(F32)).astype(BF)
        y_pass(5).start()

    def y_final():
        for i in (2, 4):
            y_pass(i).wait_recv()
        comb[YPOS, upper, :] = (yc[3, upper, :].astype(F32) + yd[0].astype(F32) + ye[0].astype(F32)).astype(BF)
        for i in (3, 5):
            y_pass(i).wait_recv()
        comb[YPOS, lower, :] = (yc[3, lower, :].astype(F32) + yd[1].astype(F32) + ye[1].astype(F32)).astype(BF)

    def second(k):
        first = x_first(k)
        later = x_second(k)
        for i in range(2):
            first[i].wait_recv()
            xs[i, k] = (comb[k, part(4 + i), :].astype(F32) + xt[1 - i, k, part(0), :].astype(F32)).astype(BF)
            later[i].start()

    def x_sum(k, half):
        x_second(k)[half].wait_recv()
        return comb[k, part(6 + half), :].astype(F32) + xt[half, k, part(1), :].astype(F32) + xf[half, k].astype(F32)

    def y_sum(jj, half, total):
        for i in range(3):
            total = total + yr[jj * 3 + i, part(half), :].astype(F32)
        return total.astype(BF)

    def final(k):
        jj, i = place(k)

        @pl.when(k == YPOS)
        def _():
            for half in range(2):
                zs[0, part(half), :] = x_sum(k, half).astype(BF)
            zr[z] = zs[0]
            to_z(0, 1).start()

        @pl.when(jnp.logical_and(k != YPOS, i != 3))
        def _():
            for half in range(2):
                ys[jj * 3 + i, part(half), :] = x_sum(k, half).astype(BF)
            to_y(jj, i).start()

        @pl.when(jnp.logical_and(k != YPOS, i == 3))
        def _():
            for n in range(3):
                to_y(jj, n).wait_recv()
            for half in range(2):
                zs[jj + 1, part(half), :] = y_sum(jj, half, x_sum(k, half))
            to_z(jj + 1, 0).start()
            to_z(jj + 1, 1).start()

    def last():
        k = NCH - 1
        for half in range(2):
            total = x_sum(k, half)
            if half == 0:
                for i in range(3):
                    to_y(2, i).wait_recv()
            zs[3, part(half), :] = y_sum(2, half, total)
            for way in range(2):
                last_z(way, half).start()

    def sent(k):
        jj, i = place(k)
        for cp in x_first(k) + x_second(k):
            cp.wait_send()

        @pl.when(k != YPOS)
        def _():
            to_partner(k).wait_send()

        @pl.when(jnp.logical_and(k != YPOS, i != 3))
        def _():
            to_y(jj, i).wait_send()

    def keys_step(m):
        dy, dz = pick([b[0] for b in BLOCKS], m), pick([b[1] for b in BLOCKS], m)
        ref = w.at[block(dy, dz, 1 - c)]
        send(ref, ref, s_w.at[m], r_w.at[m], partner).wait_recv()
        for core in range(2):
            b = block(dy, dz, core)
            cols = pl.ds(pl.multiple_of(b * BLK, BLK), BLK)
            acc[...] += jnp.dot(t[:, cols], w[b], preferred_element_type=F32)

    acc[...] = jnp.zeros_like(acc)

    def step(k, carry):
        @pl.when(jnp.logical_and(k < NCH, k != YPOS))
        def _():
            jj, i = place(k)
            gradient(k, gray(3 - i), gray(jj + 1), k % 2)

        @pl.when(jnp.logical_and(k >= 1, k < NCH + 1))
        def _():
            @pl.when(k - 1 != YPOS)
            def _():
                comb[k - 1] = both(k - 1, (k - 1) % 2)

            @pl.when(k - 1 == YPOS)
            def _():
                y_final()

            for cp in x_first(k - 1):
                cp.start()

        @pl.when(k < 4)
        def _():
            gradient(NCH + k, gray(3 - k), 0, 2 + k % 2)

        @pl.when(jnp.logical_and(k >= 1, k < 5))
        def _():
            yc[k - 1] = both(NCH + k - 1, 2 + (k - 1) % 2)

        @pl.when(k == 1)
        def _():
            y_pass(0).start()
            y_pass(1).start()

        @pl.when(k == 2)
        def _():
            y_pass(3).start()

        @pl.when(k == 3)
        def _():
            y_pass(2).start()

        @pl.when(k == YSEC)
        def _():
            y_second()

        @pl.when(k == SLOT_A)
        def _():
            ag_wait(0, 0)
            ag_start(0, 1)
            ag_start(2, 0)
            ag_start(3, 0)
            ag_wait(1, 0)
            ag_start(1, 1)
            for m in range(1, 5):
                share(m).start()

        @pl.when(k == SLOT_B0)
        def _():
            ag_wait(0, 1)
            ag_start(4, 0)
            ag_wait(2, 0)
            ag_start(2, 1)

        @pl.when(k == SLOT_B)
        def _():
            ag_wait(3, 0)
            ag_start(3, 1)
            ag_wait(1, 1)
            for m in range(5, 11):
                share(m).start()

        @pl.when(k == SLOT_C)
        def _():
            ag_wait(4, 0)
            ag_start(4, 1)
            ag_wait(2, 1)
            ag_wait(3, 1)
            for m in range(11, 15):
                share(m).start()

        @pl.when(jnp.logical_and(k >= 1 + LAG2, k < NCH + 1 + LAG2))
        def _():
            second(k - 1 - LAG2)

        @pl.when(jnp.logical_and(k >= 1 + LAGF, k < NCH + LAGF))
        def _():
            final(k - 1 - LAGF)

        @pl.when(k >= KEYS0)
        def _():
            keys_step(k - KEYS0)

        @pl.when(k >= LAGS)
        def _():
            sent(k - LAGS)

        return carry

    lax.fori_loop(0, NCH + LAGF, step, 0)
    last()
    ag_wait(4, 1)
    share(15).start()

    def keys_rest(m, carry):
        keys_step(m)
        return carry

    lax.fori_loop(NCH + LAGF - KEYS0, len(BLOCKS), keys_rest, 0)


    for q in range(4):
        lanes = pl.ds(q * 128, 128)
        keys_ref[:, lanes] = (acc[:, lanes] * rcol[...]).astype(BF)
    out_keys = pltpu.make_async_copy(keys_ref, keys_h, lsem.at[0])
    out_keys.start()

    def slot(i):
        return lax.rem(z + i, 8)

    for i in (1, 3, 4, 5, 7):
        send(zs.at[0], zr.at[slot(i)], s_z.at[0, 0], r_z.at[slot(i)], partner).wait_recv()

    def pair(i, rows):
        return zr[slot(i), rows, :].astype(F32) + zr[slot(i + 4), rows, :].astype(F32)

    everything = pl.ds(0, 128)
    ysum[...] = pair(0, everything) + pair(1, everything) + pair(3, everything)

    for half in range(2):
        rows = pl.ds(64 * half, 64)
        for way in range(2):
            last_z(way, half).wait_recv()
        fin[rows, :] = (ysum[rows, :] + pair(2, rows)).astype(BF)
        for i in (2, 1, 3):
            to_x(i, half).start()
    out_fin = pltpu.make_async_copy(fin, fin_h.at[x], lsem.at[1])
    out_fin.start()

    def waits(k, carry):
        sent(k)
        return carry

    lax.fori_loop(NCH + LAGF - LAGS, NCH, waits, 0)
    for i in range(6):
        y_pass(i).wait_send()
    for n in range(4):
        to_partner(NCH + n).wait_send()
    for h in range(2):
        for n in range(5):
            for way in range(2):
                for kind in range(2):
                    ag(h, n, way, kind).wait_send()
    for m in range(16):
        share(m).wait_send()
    for j in range(3):
        for way in range(2):
            if j or way:
                to_z(j, way).wait_send()
    for way in range(2):
        for half in range(2):
            last_z(way, half).wait_send()
    for i in range(1, 4):
        for half in range(2):
            to_x(i, half).wait_send()
    out_keys.wait()
    out_fin.wait()
    for i in range(1, 4):
        for half in range(2):
            src = lax.rem(x + i, 4)
            rows = pl.ds(64 * half, 64)
            send(fin.at[rows], fin_h.at[src, rows], s_f.at[0, half], r_f.at[src, half], xl).wait_recv()


def finish(keys_in, fin_in, gain_in, keys_out, grad_out, keys, fin, gain, grad, sems):
    s = lax.axis_index("shard")
    ins = [pltpu.make_async_copy(a, b, sems.at[i]) for i, (a, b) in enumerate([(keys_in, keys), (fin_in, fin), (gain_in, gain)])]
    for cp in ins:
        cp.start()
    ins[0].wait()
    out_keys = pltpu.make_async_copy(keys, keys_out, sems.at[3])
    out_keys.start()
    ins[1].wait()
    ins[2].wait()
    row = jnp.concatenate([gain[pl.ds(2 * s, 1), :], gain[pl.ds(2 * s + 1, 1), :]], axis=1)
    for q in range(4):
        grad[:, pl.ds(q * 128, 128)] = jnp.transpose(fin[q].astype(F32) * row)
    out_grad = pltpu.make_async_copy(grad, grad_out, sems.at[4])
    out_grad.start()
    out_keys.wait()
    out_grad.wait()


def per_device(tokens, norm_gain, codes, zero_points, scales, key_grad):
    hbm = pl.BlockSpec(memory_space=pl.ANY)
    sem = pltpu.SemaphoreType.DMA
    v = pltpu.VMEM
    norm_gain = norm_gain.reshape(64, 128)
    keys, summed = pl.pallas_call(
        kernel,
        out_shape=(jax.ShapeDtypeStruct((TOK, KV), BF), jax.ShapeDtypeStruct((4, 128, BLK), BF)),
        in_specs=[hbm] * 6,
        out_specs=(hbm, hbm),
        scratch_shapes=[
            v((TOK, D), BF), v((32, BLK, KV), BF), v((64, 128), F32), v((BLK, KV), jnp.int32), v((2, KV), jnp.int32),
            v((2, KV), F32), v((TOK, KV), BF), v((KV, TOK), F32), v((KV, TOK), BF), v((TOK, 128), F32),
            v((4, KV, BLK), F32), v((NCH + 4, KV, BLK), BF), v((NCH + 4, KV, BLK), BF), v((NCH, KV, BLK), BF),
            v((2, NCH, 128, BLK), BF), v((2, NCH, 64, BLK), BF), v((2, NCH, 64, BLK), BF),
            v((9, 128, BLK), BF), v((128, BLK), F32), v((9, 128, BLK), BF), v((4, 128, BLK), BF), v((8, 128, BLK), BF),
            v((128, BLK), BF), v((TOK, KV), F32), v((TOK, KV), BF),
            v((4, KV, BLK), BF), v((2, 256, BLK), BF), v((2, 256, BLK), BF), v((2, 256, BLK), BF), v((2, 256, BLK), BF), sem((6,)), sem((6,)),
            sem((5 + NT,)), sem((2, 2)), sem((2, 2)), sem((NCH + 4,)), sem((NCH + 4,)), sem((2, NCH)), sem((2, NCH)), sem((2, NCH)), sem((2, NCH)),
            sem((9,)), sem((9,)), sem((4, 2)), sem((8,)), sem((3, 2)), sem((4, 2)), sem((40,)), sem((40,)), sem((16,)), sem((16,)),
        ],
        compiler_params=pltpu.CompilerParams(collective_id=1, has_side_effects=True, vmem_limit_bytes=56 * 2**20),
        cost_estimate=pl.CostEstimate(flops=8 * TOK * D * KV // 2, bytes_accessed=12 * 2**20, transcendentals=TOK),
        name="layer",
    )(tokens, norm_gain, codes, zero_points, scales, key_grad)
    return pl.pallas_call(
        finish,
        out_shape=(jax.ShapeDtypeStruct((TOK, KV), BF), jax.ShapeDtypeStruct((BLK, KV), F32)),
        in_specs=[hbm] * 3,
        out_specs=(hbm, hbm),
        scratch_shapes=[v((TOK, KV), BF), v((4, 128, BLK), BF), v((64, 128), F32), v((BLK, KV), F32), sem((5,))],
        name="finish",
    )(keys, summed, norm_gain)


def solution(mesh):
    in_specs = (
        P(("grp", "shard"), None),
        P(),
        P("shard", None),
        P("shard", None),
        P("shard", None),
        P(("grp", "shard"), None),
    )
    out_specs = (P(("grp", "shard"), None), P("shard", None))
    return jax.shard_map(
        per_device, mesh=mesh, in_specs=in_specs, out_specs=out_specs, check_vma=False
    )
```

```python
import jax
import jax.numpy as jnp
from jax import lax
from jax.experimental import pallas as pl
from jax.experimental.pallas import tpu as pltpu
from jax.sharding import PartitionSpec as P

EPS = 1e-05
D, KV, TOK = 8192, 512, 512
BLK = 256
MESH = pl.DeviceIdType.MESH
BF, F32 = jnp.bfloat16, jnp.float32
ORDER = (0, 1, 3, 2)
PIECES = ((2, 0), (3, 1), (2, 1), (1, 0), (3, 0), (1, 1), (0, 0), (0, 1))
BLOCKS = [(0, 0), (0, 1), (0, 3), (1, 0), (3, 0), (0, 2), (2, 0), (1, 1), (1, 3), (3, 1), (3, 3), (1, 2), (3, 2), (2, 1), (2, 3), (2, 2)]
NCH = 13
YPOS = 10
YSEC = 7
Y0 = 2
CUT = 224
LAG2 = 2
LAGF = 5
LAGS = 8
SLOT_A = 1
SLOT_B = 7
SLOT_C = 12
SLOT_B0 = 5
KEYS0 = 8
NT = 16
FLY = 6


def gray(i):
    return i + (i // 2) * (1 - 2 * (i % 2))


def pick(table, m):
    value = table[0]
    for n in range(1, len(table)):
        value = jnp.where(m == n, table[n], value)
    return value


def kernel(tok_h, gain_h, codes_h, zp_h, sc_h, kg_h, keys_h, fin_h,
           t, w, gain, codes, zp, sc, kg, kt, rkt, rcol, own, psend, prec, comb, xt, xs, xf, ys, ysum, yr, zs, zr, fin, acc, keys_ref,
           yc, yt, yd, yu, ye, s_yy, r_yy,
           lsem, s_l, r_l, s_p, r_p, s_xt, r_xt, s_xf, r_xf, s_y, r_y, s_z, r_z, s_f, r_f, s_ag, r_ag, s_w, r_w):
    g, s = lax.axis_index("grp"), lax.axis_index("shard")
    x, zh = lax.rem(g, 4), lax.div(g, 4)
    y, zl, c = lax.div(s, 8), lax.rem(lax.div(s, 2), 4), lax.rem(s, 2)
    z = zh * 4 + zl

    def at(ax, ay, az, ac):
        ax, ay, az = lax.rem(ax, 4), lax.rem(ay, 4), lax.rem(az, 8)
        return (lax.div(az, 4) * 4 + ax, (ay * 4 + lax.rem(az, 4)) * 2 + ac)

    partner = at(x, y, z, 1 - c)
    xl, xr = at(x + 3, y, z, c), at(x + 1, y, z, c)
    hop = {("y", 0): at(x, y + 1, z, c), ("y", 1): at(x, y + 3, z, c), ("z", 0): at(x, y, z + 1, c), ("z", 1): at(x, y, z + 7, c)}

    def block(dy, dz, core):
        return (lax.rem(y + dy, 4) * 4 + lax.rem(zl + dz, 4)) * 2 + core

    def send(src, dst, ss, rs, to):
        return pltpu.make_async_remote_copy(src_ref=src, dst_ref=dst, send_sem=ss, recv_sem=rs, device_id=to, device_id_type=MESH)

    loads = [pltpu.make_async_copy(a, b, lsem.at[i]) for i, (a, b) in enumerate(
        [(codes_h, codes), (zp_h, zp), (sc_h, sc), (gain_h, gain), (kg_h, kg)])]
    for cp in loads:
        cp.start()
    rows_t = TOK // NT

    def load_t(i):
        r = pl.ds(pl.multiple_of(i * rows_t, rows_t), rows_t)
        return pltpu.make_async_copy(tok_h.at[r], t.at[r], lsem.at[5 + i])

    for i in range(FLY):
        load_t(i).start()

    barrier = pltpu.get_barrier_semaphore()
    peers = [partner] + [at(x + i, y, z, c) for i in (1, 2, 3)] + [at(x, y + i, z, c) for i in (1, 2, 3)]
    peers += [at(x, y, z + i, c) for i in range(1, 8)]
    for p in peers:
        pl.semaphore_signal(barrier, inc=1, device_id=p, device_id_type=MESH)

    for cp in loads[:4]:
        cp.wait()
    mine = block(0, 0, c)
    for j in range(2):
        row = gain[pl.ds(2 * s + j, 1), :]
        col = jnp.transpose(jnp.broadcast_to(row, (128, 128)))
        part = pl.ds(j * 128, 128)
        for q in range(4):
            lanes = pl.ds(q * 128, 128)
            shaped = (codes[part, lanes] - zp[pl.ds(j, 1), lanes]).astype(F32)
            w[mine, part, lanes] = (shaped * sc[pl.ds(j, 1), lanes] * col).astype(BF)

    pl.semaphore_wait(barrier, len(peers))

    def ag(h, n, way, kind):
        axis = ("y", "z")[(h + (n > 0)) % 2]
        dp = ORDER[n - 1] if n > 0 else 0
        off = 0 if kind == 0 else (3, 1)[way]
        if n == 0:
            dp, dq = off, 0
        else:
            dq = off
        dy, dz = (dp, dq) if h == 0 else (dq, dp)
        size = (CUT, BLK - CUT)[h]
        lo = h * CUT
        if kind == 1:
            size = size // 2
            lo = lo + size * way
        ref = w.at[block(dy, dz, c), pl.ds(lo, size)]
        i = ((h * 5 + n) * 2 + way) * 2 + kind
        return send(ref, ref, s_ag.at[i], r_ag.at[i], hop[(axis, way)])

    def ag_start(n, kind):
        for h in range(2):
            for way in range(2):
                ag(h, n, way, kind).start()

    def ag_wait(n, kind):
        for h in range(2):
            for way in range(2):
                ag(h, n, way, kind).wait_recv()

    def share(m):
        dy, dz = BLOCKS[m]
        ref = w.at[block(dy, dz, c)]
        return send(ref, ref, s_w.at[m], r_w.at[m], partner)

    ag_start(0, 0)
    ag_start(1, 0)
    share(0).start()

    loads[4].wait()
    kt[...] = jnp.transpose(kg[...].astype(F32))

    def norm_rows(i, carry):
        load_t(i).wait()

        @pl.when(i + FLY < NT)
        def _():
            load_t(i + FLY).start()

        def tile(u, carry):
            r0 = pl.multiple_of(i * rows_t + u * 16, 16)
            sums = [jnp.zeros((16, 128), F32) for _ in range(4)]
            for v in range(D // 128):
                val = t[pl.ds(r0, 16), pl.ds(v * 128, 128)].astype(F32)
                sums[v % 4] = sums[v % 4] + val * val
            total = jnp.sum((sums[0] + sums[1]) + (sums[2] + sums[3]), axis=1, keepdims=True)
            rcol[pl.ds(r0, 16), :] = jnp.broadcast_to(lax.rsqrt(total * (1.0 / D) + EPS), (16, 128))
            return carry

        return lax.fori_loop(0, rows_t // 16, tile, carry)

    lax.fori_loop(0, NT, norm_rows, 0)
    for q in range(4):
        lanes = pl.ds(q * 128, 128)
        row = jnp.transpose(rcol[lanes, :])[0:1, :]
        for i, (dx, half) in enumerate(PIECES):
            src = pl.ds(pl.multiple_of(lax.rem(x + dx, 4) * 128 + half * 64, 64), 64)
            rkt[pl.ds(i * 64, 64), lanes] = (kt[src, lanes] * row).astype(BF)

    def place(k):
        e = k - (k > YPOS).astype(jnp.int32)
        return e // 4, e % 4

    def term(b):
        cols = pl.ds(pl.multiple_of(b * BLK, BLK), BLK)
        return jnp.dot(rkt[...], t[:, cols], preferred_element_type=F32)

    def to_partner(n):
        return send(psend.at[n], prec.at[n], s_p.at[n], r_p.at[n], partner)

    def part(i):
        return pl.ds(64 * i, 64)

    def x_first(k):
        return [
            send(comb.at[k, pl.ds(0, 128)], xt.at[1, k], s_xt.at[1, k], r_xt.at[1, k], xl),
            send(comb.at[k, pl.ds(128, 128)], xt.at[0, k], s_xt.at[0, k], r_xt.at[0, k], xr),
        ]

    def x_second(k):
        return [
            send(xs.at[0, k], xf.at[0, k], s_xf.at[0, k], r_xf.at[0, k], xl),
            send(xs.at[1, k], xf.at[1, k], s_xf.at[1, k], r_xf.at[1, k], xr),
        ]

    def to_y(jj, i):
        n = jj * 3 + i
        return send(ys.at[n], yr.at[n], s_y.at[n], r_y.at[n], at(x, y + gray(3 - i), z, c))

    def to_z(j, way):
        to = at(x, y, z + gray(j) + 4 * way, c)
        return send(zs.at[j], zr.at[z], s_z.at[j, way], r_z.at[z], to)

    def last_z(way, half):
        rows = part(half)
        return send(zs.at[3, rows], zr.at[z, rows], s_l.at[way, half], r_l.at[way, half], at(x, y, z + 2 + 4 * way, c))

    def to_x(i, half):
        rows = part(half)
        return send(fin.at[rows], fin_h.at[x, rows], s_f.at[i - 1, half], r_f.at[x, half], at(x + i, y, z, c))

    def gradient(n, dy, dz, held):
        psend[n] = term(block(dy, dz, 1 - c)).astype(BF)
        to_partner(n).start()
        own[held] = term(block(dy, dz, c))

    def both(n, held):
        to_partner(n).wait_recv()
        return (own[held] + prec[n].astype(F32)).astype(BF)

    upper, lower = pl.ds(0, 256), pl.ds(256, 256)

    def y_pass(i):
        src, dst, way = (
            (yc.at[0, upper], yt.at[0], 1),
            (yc.at[0, lower], yt.at[1], 0),
            (yc.at[2, upper], yd.at[0], 0),
            (yc.at[1, lower], yd.at[1], 1),
            (yu.at[0], ye.at[0], 1),
            (yu.at[1], ye.at[1], 0),
        )[i]
        return send(src, dst, s_yy.at[i], r_yy.at[i], hop[("y", way)])

    def y_second():
        y_pass(0).wait_recv()
        yu[0] = (yc[1, upper, :].astype(F32) + yt[0].astype(F32)).astype(BF)
        y_pass(4).start()
        y_pass(1).wait_recv()
        yu[1] = (yc[2, lower, :].astype(F32) + yt[1].astype(F32)).astype(BF)
        y_pass(5).start()

    def y_final():
        for i in (2, 4):
            y_pass(i).wait_recv()
        comb[YPOS, upper, :] = (yc[3, upper, :].astype(F32) + yd[0].astype(F32) + ye[0].astype(F32)).astype(BF)
        for i in (3, 5):
            y_pass(i).wait_recv()
        comb[YPOS, lower, :] = (yc[3, lower, :].astype(F32) + yd[1].astype(F32) + ye[1].astype(F32)).astype(BF)

    def second(k):
        first = x_first(k)
        later = x_second(k)
        for i in range(2):
            first[i].wait_recv()
            xs[i, k] = (comb[k, part(4 + i), :].astype(F32) + xt[1 - i, k, part(0), :].astype(F32)).astype(BF)
            later[i].start()

    def x_sum(k, half):
        x_second(k)[half].wait_recv()
        return comb[k, part(6 + half), :].astype(F32) + xt[half, k, part(1), :].astype(F32) + xf[half, k].astype(F32)

    def y_sum(jj, half, total):
        for i in range(3):
            total = total + yr[jj * 3 + i, part(half), :].astype(F32)
        return total.astype(BF)

    def final(k):
        jj, i = place(k)

        @pl.when(k == YPOS)
        def _():
            for half in range(2):
                zs[0, part(half), :] = x_sum(k, half).astype(BF)
            zr[z] = zs[0]
            to_z(0, 1).start()

        @pl.when(jnp.logical_and(k != YPOS, i != 3))
        def _():
            for half in range(2):
                ys[jj * 3 + i, part(half), :] = x_sum(k, half).astype(BF)
            to_y(jj, i).start()

        @pl.when(jnp.logical_and(k != YPOS, i == 3))
        def _():
            for n in range(3):
                to_y(jj, n).wait_recv()
            for half in range(2):
                zs[jj + 1, part(half), :] = y_sum(jj, half, x_sum(k, half))
            to_z(jj + 1, 0).start()
            to_z(jj + 1, 1).start()

    def last():
        k = NCH - 1
        for half in range(2):
            total = x_sum(k, half)
            if half == 0:
                for i in range(3):
                    to_y(2, i).wait_recv()
            zs[3, part(half), :] = y_sum(2, half, total)
            for way in range(2):
                last_z(way, half).start()

    def sent(k):
        jj, i = place(k)
        for cp in x_first(k) + x_second(k):
            cp.wait_send()

        @pl.when(k != YPOS)
        def _():
            to_partner(k).wait_send()

        @pl.when(jnp.logical_and(k != YPOS, i != 3))
        def _():
            to_y(jj, i).wait_send()

    def keys_step(m):
        dy, dz = pick([b[0] for b in BLOCKS], m), pick([b[1] for b in BLOCKS], m)
        ref = w.at[block(dy, dz, 1 - c)]
        send(ref, ref, s_w.at[m], r_w.at[m], partner).wait_recv()
        b = block(dy, dz, 0)
        cols = pl.ds(pl.multiple_of(b * BLK, 2 * BLK), 2 * BLK)
        acc[...] += jnp.dot(t[:, cols], w[pl.ds(b, 2)].reshape(2 * BLK, KV), preferred_element_type=F32)

    acc[...] = jnp.zeros_like(acc)

    def step(k, carry):
        @pl.when(jnp.logical_and(k < NCH, k != YPOS))
        def _():
            jj, i = place(k)
            gradient(k, gray(3 - i), gray(jj + 1), k % 2)

        @pl.when(jnp.logical_and(k >= 1, k < NCH + 1))
        def _():
            @pl.when(k - 1 != YPOS)
            def _():
                comb[k - 1] = both(k - 1, (k - 1) % 2)

            @pl.when(k - 1 == YPOS)
            def _():
                y_final()

            for cp in x_first(k - 1):
                cp.start()

        @pl.when(jnp.logical_and(k >= Y0, k < Y0 + 4))
        def _():
            i = k - Y0
            gradient(NCH + i, gray(3 - i), 0, 2 + i % 2)

        @pl.when(jnp.logical_and(k >= Y0 + 1, k < Y0 + 5))
        def _():
            i = k - Y0 - 1
            yc[i] = both(NCH + i, 2 + i % 2)

        @pl.when(k == Y0 + 1)
        def _():
            y_pass(0).start()
            y_pass(1).start()

        @pl.when(k == Y0 + 2)
        def _():
            y_pass(3).start()

        @pl.when(k == Y0 + 3)
        def _():
            y_pass(2).start()

        @pl.when(k == YSEC)
        def _():
            y_second()

        @pl.when(k == SLOT_A)
        def _():
            ag_wait(0, 0)
            ag_start(0, 1)
            ag_start(2, 0)
            ag_start(3, 0)
            ag_wait(1, 0)
            ag_start(1, 1)
            for m in range(1, 5):
                share(m).start()

        @pl.when(k == SLOT_B0)
        def _():
            ag_wait(0, 1)
            ag_start(4, 0)
            ag_wait(2, 0)
            ag_start(2, 1)

        @pl.when(k == SLOT_B)
        def _():
            ag_wait(3, 0)
            ag_start(3, 1)
            ag_wait(1, 1)
            for m in range(5, 11):
                share(m).start()

        @pl.when(k == SLOT_C)
        def _():
            ag_wait(4, 0)
            ag_start(4, 1)
            ag_wait(2, 1)
            ag_wait(3, 1)
            for m in range(11, 15):
                share(m).start()

        @pl.when(jnp.logical_and(k >= 1 + LAG2, k < NCH + 1 + LAG2))
        def _():
            second(k - 1 - LAG2)

        @pl.when(jnp.logical_and(k >= 1 + LAGF, k < NCH + LAGF))
        def _():
            final(k - 1 - LAGF)

        @pl.when(k >= KEYS0)
        def _():
            keys_step(k - KEYS0)

        @pl.when(k >= LAGS)
        def _():
            sent(k - LAGS)

        return carry

    lax.fori_loop(0, NCH + LAGF, step, 0)
    last()
    ag_wait(4, 1)
    share(15).start()

    def keys_rest(m, carry):
        keys_step(m)
        return carry

    lax.fori_loop(NCH + LAGF - KEYS0, len(BLOCKS), keys_rest, 0)


    for q in range(4):
        lanes = pl.ds(q * 128, 128)
        keys_ref[:, lanes] = (acc[:, lanes] * rcol[...]).astype(BF)
    out_keys = pltpu.make_async_copy(keys_ref, keys_h, lsem.at[0])
    out_keys.start()

    def slot(i):
        return lax.rem(z + i, 8)

    for i in (1, 3, 4, 5, 7):
        send(zs.at[0], zr.at[slot(i)], s_z.at[0, 0], r_z.at[slot(i)], partner).wait_recv()

    def pair(i, rows):
        return zr[slot(i), rows, :].astype(F32) + zr[slot(i + 4), rows, :].astype(F32)

    everything = pl.ds(0, 128)
    ysum[...] = pair(0, everything) + pair(1, everything) + pair(3, everything)

    for half in range(2):
        rows = pl.ds(64 * half, 64)
        for way in range(2):
            last_z(way, half).wait_recv()
        fin[rows, :] = (ysum[rows, :] + pair(2, rows)).astype(BF)
        for i in (2, 1, 3):
            to_x(i, half).start()
    out_fin = pltpu.make_async_copy(fin, fin_h.at[x], lsem.at[1])
    out_fin.start()

    def waits(k, carry):
        sent(k)
        return carry

    lax.fori_loop(NCH + LAGF - LAGS, NCH, waits, 0)
    for i in range(6):
        y_pass(i).wait_send()
    for n in range(4):
        to_partner(NCH + n).wait_send()
    for h in range(2):
        for n in range(5):
            for way in range(2):
                for kind in range(2):
                    ag(h, n, way, kind).wait_send()
    for m in range(16):
        share(m).wait_send()
    for j in range(3):
        for way in range(2):
            if j or way:
                to_z(j, way).wait_send()
    for way in range(2):
        for half in range(2):
            last_z(way, half).wait_send()
    for i in range(1, 4):
        for half in range(2):
            to_x(i, half).wait_send()
    out_keys.wait()
    out_fin.wait()
    for i in range(1, 4):
        for half in range(2):
            src = lax.rem(x + i, 4)
            rows = pl.ds(64 * half, 64)
            send(fin.at[rows], fin_h.at[src, rows], s_f.at[0, half], r_f.at[src, half], xl).wait_recv()


def finish(keys_in, fin_in, gain_in, keys_out, grad_out, keys, fin, gain, grad, sems):
    s = lax.axis_index("shard")
    ins = [pltpu.make_async_copy(a, b, sems.at[i]) for i, (a, b) in enumerate([(fin_in, fin), (gain_in, gain), (keys_in, keys)])]
    for cp in ins:
        cp.start()
    ins[0].wait()
    ins[1].wait()
    row = jnp.concatenate([gain[pl.ds(2 * s, 1), :], gain[pl.ds(2 * s + 1, 1), :]], axis=1)
    outs = []
    for q in range(4):
        lanes = pl.ds(q * 128, 128)
        grad[:, lanes] = jnp.transpose(fin[q].astype(F32) * row)
        outs.append(pltpu.make_async_copy(grad.at[:, lanes], grad_out.at[:, lanes], sems.at[3 + q]))
        outs[-1].start()
        if q == 1:
            ins[2].wait()
            outs.append(pltpu.make_async_copy(keys, keys_out, sems.at[7]))
            outs[-1].start()
    for cp in outs:
        cp.wait()


def per_device(tokens, norm_gain, codes, zero_points, scales, key_grad):
    hbm = pl.BlockSpec(memory_space=pl.ANY)
    sem = pltpu.SemaphoreType.DMA
    v = pltpu.VMEM
    norm_gain = norm_gain.reshape(64, 128)
    keys, summed = pl.pallas_call(
        kernel,
        out_shape=(jax.ShapeDtypeStruct((TOK, KV), BF), jax.ShapeDtypeStruct((4, 128, BLK), BF)),
        in_specs=[hbm] * 6,
        out_specs=(hbm, hbm),
        scratch_shapes=[
            v((TOK, D), BF), v((32, BLK, KV), BF), v((64, 128), F32), v((BLK, KV), jnp.int32), v((2, KV), jnp.int32),
            v((2, KV), F32), v((TOK, KV), BF), v((KV, TOK), F32), v((KV, TOK), BF), v((TOK, 128), F32),
            v((4, KV, BLK), F32), v((NCH + 4, KV, BLK), BF), v((NCH + 4, KV, BLK), BF), v((NCH, KV, BLK), BF),
            v((2, NCH, 128, BLK), BF), v((2, NCH, 64, BLK), BF), v((2, NCH, 64, BLK), BF),
            v((9, 128, BLK), BF), v((128, BLK), F32), v((9, 128, BLK), BF), v((4, 128, BLK), BF), v((8, 128, BLK), BF),
            v((128, BLK), BF), v((TOK, KV), F32), v((TOK, KV), BF),
            v((4, KV, BLK), BF), v((2, 256, BLK), BF), v((2, 256, BLK), BF), v((2, 256, BLK), BF), v((2, 256, BLK), BF), sem((6,)), sem((6,)),
            sem((5 + NT,)), sem((2, 2)), sem((2, 2)), sem((NCH + 4,)), sem((NCH + 4,)), sem((2, NCH)), sem((2, NCH)), sem((2, NCH)), sem((2, NCH)),
            sem((9,)), sem((9,)), sem((4, 2)), sem((8,)), sem((3, 2)), sem((4, 2)), sem((40,)), sem((40,)), sem((16,)), sem((16,)),
        ],
        compiler_params=pltpu.CompilerParams(collective_id=1, has_side_effects=True, vmem_limit_bytes=56 * 2**20),
        cost_estimate=pl.CostEstimate(flops=8 * TOK * D * KV // 2, bytes_accessed=12 * 2**20, transcendentals=TOK),
        name="layer",
    )(tokens, norm_gain, codes, zero_points, scales, key_grad)
    return pl.pallas_call(
        finish,
        out_shape=(jax.ShapeDtypeStruct((TOK, KV), BF), jax.ShapeDtypeStruct((BLK, KV), F32)),
        in_specs=[hbm] * 3,
        out_specs=(hbm, hbm),
        scratch_shapes=[v((TOK, KV), BF), v((4, 128, BLK), BF), v((64, 128), F32), v((BLK, KV), F32), sem((8,))],
        name="finish",
    )(keys, summed, norm_gain)


def solution(mesh):
    in_specs = (
        P(("grp", "shard"), None),
        P(),
        P("shard", None),
        P("shard", None),
        P("shard", None),
        P(("grp", "shard"), None),
    )
    out_specs = (P(("grp", "shard"), None), P("shard", None))
    return jax.shard_map(
        per_device, mesh=mesh, in_specs=in_specs, out_specs=out_specs, check_vma=False
    )
```

```python
import jax
import jax.numpy as jnp
from jax import lax
from jax.experimental import pallas as pl
from jax.experimental.pallas import tpu as pltpu
from jax.sharding import PartitionSpec as P

EPS = 1e-05
D, KV, TOK = 8192, 512, 512
BLK = 256
MESH = pl.DeviceIdType.MESH
BF, F32 = jnp.bfloat16, jnp.float32
ORDER = (0, 1, 3, 2)
PIECES = ((2, 0), (3, 1), (2, 1), (1, 0), (3, 0), (1, 1), (0, 0), (0, 1))
BLOCKS = [(0, 0), (0, 1), (0, 3), (1, 0), (3, 0), (0, 2), (2, 0), (1, 1), (1, 3), (3, 1), (3, 3), (1, 2), (3, 2), (2, 1), (2, 3), (2, 2)]
NCH = 13
YPOS = 10
YSEC = 7
Y0 = 2
CUT = 224
LAG2 = 2
LAGF = 5
LAGS = 8
SLOT_A = 1
SLOT_B = 7
SLOT_C = 12
SLOT_B0 = 4
KEYS0 = 8
NT = 16
FLY = 8


def gray(i):
    return i + (i // 2) * (1 - 2 * (i % 2))


def pick(table, m):
    value = table[0]
    for n in range(1, len(table)):
        value = jnp.where(m == n, table[n], value)
    return value


def kernel(tok_h, gain_h, codes_h, zp_h, sc_h, kg_h, keys_h, fin_h,
           t, w, gain, codes, zp, sc, kg, kt, rkt, rcol, own, psend, prec, comb, xt, xs, xf, ys, ysum, yr, zs, zr, fin, acc, keys_ref,
           yc, yt, yd, yu, ye, s_yy, r_yy,
           lsem, s_l, r_l, s_p, r_p, s_xt, r_xt, s_xf, r_xf, s_y, r_y, s_z, r_z, s_f, r_f, s_ag, r_ag, s_w, r_w):
    g, s = lax.axis_index("grp"), lax.axis_index("shard")
    x, zh = lax.rem(g, 4), lax.div(g, 4)
    y, zl, c = lax.div(s, 8), lax.rem(lax.div(s, 2), 4), lax.rem(s, 2)
    z = zh * 4 + zl

    def at(ax, ay, az, ac):
        ax, ay, az = lax.rem(ax, 4), lax.rem(ay, 4), lax.rem(az, 8)
        return (lax.div(az, 4) * 4 + ax, (ay * 4 + lax.rem(az, 4)) * 2 + ac)

    partner = at(x, y, z, 1 - c)
    xl, xr = at(x + 3, y, z, c), at(x + 1, y, z, c)
    hop = {("y", 0): at(x, y + 1, z, c), ("y", 1): at(x, y + 3, z, c), ("z", 0): at(x, y, z + 1, c), ("z", 1): at(x, y, z + 7, c)}

    def block(dy, dz, core):
        return (lax.rem(y + dy, 4) * 4 + lax.rem(zl + dz, 4)) * 2 + core

    def send(src, dst, ss, rs, to):
        return pltpu.make_async_remote_copy(src_ref=src, dst_ref=dst, send_sem=ss, recv_sem=rs, device_id=to, device_id_type=MESH)

    loads = [pltpu.make_async_copy(a, b, lsem.at[i]) for i, (a, b) in enumerate(
        [(codes_h, codes), (zp_h, zp), (sc_h, sc), (gain_h, gain), (kg_h, kg)])]
    for cp in loads:
        cp.start()
    rows_t = TOK // NT

    def load_t(i):
        r = pl.ds(pl.multiple_of(i * rows_t, rows_t), rows_t)
        return pltpu.make_async_copy(tok_h.at[r], t.at[r], lsem.at[5 + i])

    for i in range(FLY):
        load_t(i).start()

    barrier = pltpu.get_barrier_semaphore()
    peers = [partner] + [at(x + i, y, z, c) for i in (1, 2, 3)] + [at(x, y + i, z, c) for i in (1, 2, 3)]
    peers += [at(x, y, z + i, c) for i in range(1, 8)]
    for p in peers:
        pl.semaphore_signal(barrier, inc=1, device_id=p, device_id_type=MESH)

    for cp in loads[:4]:
        cp.wait()
    mine = block(0, 0, c)
    for j in range(2):
        row = gain[pl.ds(2 * s + j, 1), :]
        col = jnp.transpose(jnp.broadcast_to(row, (128, 128)))
        part = pl.ds(j * 128, 128)
        for q in range(4):
            lanes = pl.ds(q * 128, 128)
            shaped = (codes[part, lanes] - zp[pl.ds(j, 1), lanes]).astype(F32)
            w[mine, part, lanes] = (shaped * sc[pl.ds(j, 1), lanes] * col).astype(BF)

    pl.semaphore_wait(barrier, len(peers))

    def ag(h, n, way, kind):
        axis = ("y", "z")[(h + (n > 0)) % 2]
        dp = ORDER[n - 1] if n > 0 else 0
        off = 0 if kind == 0 else (3, 1)[way]
        if n == 0:
            dp, dq = off, 0
        else:
            dq = off
        dy, dz = (dp, dq) if h == 0 else (dq, dp)
        size = (CUT, BLK - CUT)[h]
        lo = h * CUT
        if kind == 1:
            size = size // 2
            lo = lo + size * way
        ref = w.at[block(dy, dz, c), pl.ds(lo, size)]
        i = ((h * 5 + n) * 2 + way) * 2 + kind
        return send(ref, ref, s_ag.at[i], r_ag.at[i], hop[(axis, way)])

    def ag_start(n, kind):
        for h in range(2):
            for way in range(2):
                ag(h, n, way, kind).start()

    def ag_wait(n, kind):
        for h in range(2):
            for way in range(2):
                ag(h, n, way, kind).wait_recv()

    def share(m):
        dy, dz = BLOCKS[m]
        ref = w.at[block(dy, dz, c)]
        return send(ref, ref, s_w.at[m], r_w.at[m], partner)

    ag_start(0, 0)
    ag_start(1, 0)
    share(0).start()

    loads[4].wait()
    kt[...] = jnp.transpose(kg[...].astype(F32))

    def norm_rows(i, carry):
        load_t(i).wait()

        @pl.when(i + FLY < NT)
        def _():
            load_t(i + FLY).start()

        def tile(u, carry):
            r0 = pl.multiple_of(i * rows_t + u * 16, 16)
            sums = [jnp.zeros((16, 128), F32) for _ in range(4)]
            for v in range(D // 128):
                val = t[pl.ds(r0, 16), pl.ds(v * 128, 128)].astype(F32)
                sums[v % 4] = sums[v % 4] + val * val
            total = jnp.sum((sums[0] + sums[1]) + (sums[2] + sums[3]), axis=1, keepdims=True)
            rcol[pl.ds(r0, 16), :] = jnp.broadcast_to(lax.rsqrt(total * (1.0 / D) + EPS), (16, 128))
            return carry

        return lax.fori_loop(0, rows_t // 16, tile, carry)

    lax.fori_loop(0, NT, norm_rows, 0)
    for q in range(4):
        lanes = pl.ds(q * 128, 128)
        row = jnp.transpose(rcol[lanes, :])[0:1, :]
        for i, (dx, half) in enumerate(PIECES):
            src = pl.ds(pl.multiple_of(lax.rem(x + dx, 4) * 128 + half * 64, 64), 64)
            rkt[pl.ds(i * 64, 64), lanes] = (kt[src, lanes] * row).astype(BF)

    def place(k):
        e = k - (k > YPOS).astype(jnp.int32)
        return e // 4, e % 4

    def term(b):
        cols = pl.ds(pl.multiple_of(b * BLK, BLK), BLK)
        return jnp.dot(rkt[...], t[:, cols], preferred_element_type=F32)

    def to_partner(n):
        return send(psend.at[n], prec.at[n], s_p.at[n], r_p.at[n], partner)

    def part(i):
        return pl.ds(64 * i, 64)

    def x_first(k):
        return [
            send(comb.at[k, pl.ds(0, 128)], xt.at[1, k], s_xt.at[1, k], r_xt.at[1, k], xl),
            send(comb.at[k, pl.ds(128, 128)], xt.at[0, k], s_xt.at[0, k], r_xt.at[0, k], xr),
        ]

    def x_second(k):
        return [
            send(xs.at[0, k], xf.at[0, k], s_xf.at[0, k], r_xf.at[0, k], xl),
            send(xs.at[1, k], xf.at[1, k], s_xf.at[1, k], r_xf.at[1, k], xr),
        ]

    def to_y(jj, i):
        n = jj * 3 + i
        return send(ys.at[n], yr.at[n], s_y.at[n], r_y.at[n], at(x, y + gray(3 - i), z, c))

    def to_z(j, way):
        to = at(x, y, z + gray(j) + 4 * way, c)
        return send(zs.at[j], zr.at[z], s_z.at[j, way], r_z.at[z], to)

    def last_z(way, half):
        rows = part(half)
        return send(zs.at[3, rows], zr.at[z, rows], s_l.at[way, half], r_l.at[way, half], at(x, y, z + 2 + 4 * way, c))

    def to_x(i, half):
        rows = part(half)
        return send(fin.at[rows], fin_h.at[x, rows], s_f.at[i - 1, half], r_f.at[x, half], at(x + i, y, z, c))

    def gradient(n, dy, dz, held):
        psend[n] = term(block(dy, dz, 1 - c)).astype(BF)
        to_partner(n).start()
        own[held] = term(block(dy, dz, c))

    def both(n, held):
        to_partner(n).wait_recv()
        return (own[held] + prec[n].astype(F32)).astype(BF)

    upper, lower = pl.ds(0, 256), pl.ds(256, 256)

    def y_pass(i):
        src, dst, way = (
            (yc.at[0, upper], yt.at[0], 1),
            (yc.at[0, lower], yt.at[1], 0),
            (yc.at[2, upper], yd.at[0], 0),
            (yc.at[1, lower], yd.at[1], 1),
            (yu.at[0], ye.at[0], 1),
            (yu.at[1], ye.at[1], 0),
        )[i]
        return send(src, dst, s_yy.at[i], r_yy.at[i], hop[("y", way)])

    def y_second():
        y_pass(0).wait_recv()
        yu[0] = (yc[1, upper, :].astype(F32) + yt[0].astype(F32)).astype(BF)
        y_pass(4).start()
        y_pass(1).wait_recv()
        yu[1] = (yc[2, lower, :].astype(F32) + yt[1].astype(F32)).astype(BF)
        y_pass(5).start()

    def y_final():
        for i in (2, 4):
            y_pass(i).wait_recv()
        comb[YPOS, upper, :] = (yc[3, upper, :].astype(F32) + yd[0].astype(F32) + ye[0].astype(F32)).astype(BF)
        for i in (3, 5):
            y_pass(i).wait_recv()
        comb[YPOS, lower, :] = (yc[3, lower, :].astype(F32) + yd[1].astype(F32) + ye[1].astype(F32)).astype(BF)

    def second(k):
        first = x_first(k)
        later = x_second(k)
        for i in range(2):
            first[i].wait_recv()
            xs[i, k] = (comb[k, part(4 + i), :].astype(F32) + xt[1 - i, k, part(0), :].astype(F32)).astype(BF)
            later[i].start()

    def x_sum(k, half):
        x_second(k)[half].wait_recv()
        return comb[k, part(6 + half), :].astype(F32) + xt[half, k, part(1), :].astype(F32) + xf[half, k].astype(F32)

    def y_sum(jj, half, total):
        for i in range(3):
            total = total + yr[jj * 3 + i, part(half), :].astype(F32)
        return total.astype(BF)

    def final(k):
        jj, i = place(k)

        @pl.when(k == YPOS)
        def _():
            for half in range(2):
                zs[0, part(half), :] = x_sum(k, half).astype(BF)
            zr[z] = zs[0]
            to_z(0, 1).start()

        @pl.when(jnp.logical_and(k != YPOS, i != 3))
        def _():
            for half in range(2):
                ys[jj * 3 + i, part(half), :] = x_sum(k, half).astype(BF)
            to_y(jj, i).start()

        @pl.when(jnp.logical_and(k != YPOS, i == 3))
        def _():
            for n in range(3):
                to_y(jj, n).wait_recv()
            for half in range(2):
                zs[jj + 1, part(half), :] = y_sum(jj, half, x_sum(k, half))
            to_z(jj + 1, 0).start()
            to_z(jj + 1, 1).start()

    def last():
        k = NCH - 1
        for half in range(2):
            total = x_sum(k, half)
            if half == 0:
                for i in range(3):
                    to_y(2, i).wait_recv()
            zs[3, part(half), :] = y_sum(2, half, total)
            for way in range(2):
                last_z(way, half).start()

    def sent(k):
        jj, i = place(k)
        for cp in x_first(k) + x_second(k):
            cp.wait_send()

        @pl.when(k != YPOS)
        def _():
            to_partner(k).wait_send()

        @pl.when(jnp.logical_and(k != YPOS, i != 3))
        def _():
            to_y(jj, i).wait_send()

    def keys_step(m):
        dy, dz = pick([b[0] for b in BLOCKS], m), pick([b[1] for b in BLOCKS], m)
        ref = w.at[block(dy, dz, 1 - c)]
        send(ref, ref, s_w.at[m], r_w.at[m], partner).wait_recv()
        b = block(dy, dz, 0)
        cols = pl.ds(pl.multiple_of(b * BLK, 2 * BLK), 2 * BLK)
        acc[...] += jnp.dot(t[:, cols], w[pl.ds(b, 2)].reshape(2 * BLK, KV), preferred_element_type=F32)

    acc[...] = jnp.zeros_like(acc)

    def step(k, carry):
        @pl.when(jnp.logical_and(k < NCH, k != YPOS))
        def _():
            jj, i = place(k)
            gradient(k, gray(3 - i), gray(jj + 1), k % 2)

        @pl.when(jnp.logical_and(k >= 1, k < NCH + 1))
        def _():
            @pl.when(k - 1 != YPOS)
            def _():
                comb[k - 1] = both(k - 1, (k - 1) % 2)

            @pl.when(k - 1 == YPOS)
            def _():
                y_final()

            for cp in x_first(k - 1):
                cp.start()

        @pl.when(jnp.logical_and(k >= Y0, k < Y0 + 4))
        def _():
            i = k - Y0
            gradient(NCH + i, gray(3 - i), 0, 2 + i % 2)

        @pl.when(jnp.logical_and(k >= Y0 + 1, k < Y0 + 5))
        def _():
            i = k - Y0 - 1
            yc[i] = both(NCH + i, 2 + i % 2)

        @pl.when(k == Y0 + 1)
        def _():
            y_pass(0).start()
            y_pass(1).start()

        @pl.when(k == Y0 + 2)
        def _():
            y_pass(3).start()

        @pl.when(k == Y0 + 3)
        def _():
            y_pass(2).start()

        @pl.when(k == YSEC)
        def _():
            y_second()

        @pl.when(k == SLOT_A)
        def _():
            ag_wait(0, 0)
            ag_start(0, 1)
            ag_start(2, 0)
            ag_start(3, 0)
            ag_wait(1, 0)
            ag_start(1, 1)
            for m in range(1, 5):
                share(m).start()

        @pl.when(k == SLOT_B0)
        def _():
            ag_wait(0, 1)
            ag_start(4, 0)
            ag_wait(2, 0)
            ag_start(2, 1)

        @pl.when(k == SLOT_B)
        def _():
            ag_wait(3, 0)
            ag_start(3, 1)
            ag_wait(1, 1)
            for m in range(5, 11):
                share(m).start()

        @pl.when(k == SLOT_C)
        def _():
            ag_wait(4, 0)
            ag_start(4, 1)
            ag_wait(2, 1)
            ag_wait(3, 1)
            for m in range(11, 15):
                share(m).start()

        @pl.when(jnp.logical_and(k >= 1 + LAG2, k < NCH + 1 + LAG2))
        def _():
            second(k - 1 - LAG2)

        @pl.when(jnp.logical_and(k >= 1 + LAGF, k < NCH + LAGF))
        def _():
            final(k - 1 - LAGF)

        @pl.when(k >= KEYS0)
        def _():
            keys_step(k - KEYS0)

        @pl.when(k >= LAGS)
        def _():
            sent(k - LAGS)

        return carry

    lax.fori_loop(0, NCH + LAGF, step, 0)
    last()
    ag_wait(4, 1)
    share(15).start()

    def keys_rest(m, carry):
        keys_step(m)
        return carry

    lax.fori_loop(NCH + LAGF - KEYS0, len(BLOCKS), keys_rest, 0)


    for q in range(4):
        lanes = pl.ds(q * 128, 128)
        keys_ref[:, lanes] = (acc[:, lanes] * rcol[...]).astype(BF)
    out_keys = pltpu.make_async_copy(keys_ref, keys_h, lsem.at[0])
    out_keys.start()

    def slot(i):
        return lax.rem(z + i, 8)

    for i in (1, 3, 4, 5, 7):
        send(zs.at[0], zr.at[slot(i)], s_z.at[0, 0], r_z.at[slot(i)], partner).wait_recv()

    def pair(i, rows):
        return zr[slot(i), rows, :].astype(F32) + zr[slot(i + 4), rows, :].astype(F32)

    everything = pl.ds(0, 128)
    ysum[...] = pair(0, everything) + pair(1, everything) + pair(3, everything)

    for half in range(2):
        rows = pl.ds(64 * half, 64)
        for way in range(2):
            last_z(way, half).wait_recv()
        fin[rows, :] = (ysum[rows, :] + pair(2, rows)).astype(BF)
        for i in (2, 1, 3):
            to_x(i, half).start()
    out_fin = pltpu.make_async_copy(fin, fin_h.at[x], lsem.at[1])
    out_fin.start()

    def waits(k, carry):
        sent(k)
        return carry

    lax.fori_loop(NCH + LAGF - LAGS, NCH, waits, 0)
    for i in range(6):
        y_pass(i).wait_send()
    for n in range(4):
        to_partner(NCH + n).wait_send()
    for h in range(2):
        for n in range(5):
            for way in range(2):
                for kind in range(2):
                    ag(h, n, way, kind).wait_send()
    for m in range(16):
        share(m).wait_send()
    for j in range(3):
        for way in range(2):
            if j or way:
                to_z(j, way).wait_send()
    for way in range(2):
        for half in range(2):
            last_z(way, half).wait_send()
    for i in range(1, 4):
        for half in range(2):
            to_x(i, half).wait_send()
    out_keys.wait()
    out_fin.wait()
    for i in range(1, 4):
        for half in range(2):
            src = lax.rem(x + i, 4)
            rows = pl.ds(64 * half, 64)
            send(fin.at[rows], fin_h.at[src, rows], s_f.at[0, half], r_f.at[src, half], xl).wait_recv()


def finish(keys_in, fin_in, gain_in, keys_out, grad_out, keys, fin, gain, grad, sems):
    s = lax.axis_index("shard")
    ins = [pltpu.make_async_copy(a, b, sems.at[i]) for i, (a, b) in enumerate([(fin_in, fin), (gain_in, gain), (keys_in, keys)])]
    for cp in ins:
        cp.start()
    ins[0].wait()
    ins[1].wait()
    row = jnp.concatenate([gain[pl.ds(2 * s, 1), :], gain[pl.ds(2 * s + 1, 1), :]], axis=1)
    outs = []
    for q in range(4):
        lanes = pl.ds(q * 128, 128)
        grad[:, lanes] = jnp.transpose(fin[q].astype(F32) * row)
        outs.append(pltpu.make_async_copy(grad.at[:, lanes], grad_out.at[:, lanes], sems.at[3 + q]))
        outs[-1].start()
        if q == 1:
            ins[2].wait()
            outs.append(pltpu.make_async_copy(keys, keys_out, sems.at[7]))
            outs[-1].start()
    for cp in outs:
        cp.wait()


def per_device(tokens, norm_gain, codes, zero_points, scales, key_grad):
    hbm = pl.BlockSpec(memory_space=pl.ANY)
    sem = pltpu.SemaphoreType.DMA
    v = pltpu.VMEM
    norm_gain = norm_gain.reshape(64, 128)
    keys, summed = pl.pallas_call(
        kernel,
        out_shape=(jax.ShapeDtypeStruct((TOK, KV), BF), jax.ShapeDtypeStruct((4, 128, BLK), BF)),
        in_specs=[hbm] * 6,
        out_specs=(hbm, hbm),
        scratch_shapes=[
            v((TOK, D), BF), v((32, BLK, KV), BF), v((64, 128), F32), v((BLK, KV), jnp.int32), v((2, KV), jnp.int32),
            v((2, KV), F32), v((TOK, KV), BF), v((KV, TOK), F32), v((KV, TOK), BF), v((TOK, 128), F32),
            v((4, KV, BLK), F32), v((NCH + 4, KV, BLK), BF), v((NCH + 4, KV, BLK), BF), v((NCH, KV, BLK), BF),
            v((2, NCH, 128, BLK), BF), v((2, NCH, 64, BLK), BF), v((2, NCH, 64, BLK), BF),
            v((9, 128, BLK), BF), v((128, BLK), F32), v((9, 128, BLK), BF), v((4, 128, BLK), BF), v((8, 128, BLK), BF),
            v((128, BLK), BF), v((TOK, KV), F32), v((TOK, KV), BF),
            v((4, KV, BLK), BF), v((2, 256, BLK), BF), v((2, 256, BLK), BF), v((2, 256, BLK), BF), v((2, 256, BLK), BF), sem((6,)), sem((6,)),
            sem((5 + NT,)), sem((2, 2)), sem((2, 2)), sem((NCH + 4,)), sem((NCH + 4,)), sem((2, NCH)), sem((2, NCH)), sem((2, NCH)), sem((2, NCH)),
            sem((9,)), sem((9,)), sem((4, 2)), sem((8,)), sem((3, 2)), sem((4, 2)), sem((40,)), sem((40,)), sem((16,)), sem((16,)),
        ],
        compiler_params=pltpu.CompilerParams(collective_id=1, has_side_effects=True, vmem_limit_bytes=56 * 2**20),
        cost_estimate=pl.CostEstimate(flops=8 * TOK * D * KV // 2, bytes_accessed=12 * 2**20, transcendentals=TOK),
        name="layer",
    )(tokens, norm_gain, codes, zero_points, scales, key_grad)
    return pl.pallas_call(
        finish,
        out_shape=(jax.ShapeDtypeStruct((TOK, KV), BF), jax.ShapeDtypeStruct((BLK, KV), F32)),
        in_specs=[hbm] * 3,
        out_specs=(hbm, hbm),
        scratch_shapes=[v((TOK, KV), BF), v((4, 128, BLK), BF), v((64, 128), F32), v((BLK, KV), F32), sem((8,))],
        name="finish",
    )(keys, summed, norm_gain)


def solution(mesh):
    in_specs = (
        P(("grp", "shard"), None),
        P(),
        P("shard", None),
        P("shard", None),
        P("shard", None),
        P(("grp", "shard"), None),
    )
    out_specs = (P(("grp", "shard"), None), P("shard", None))
    return jax.shard_map(
        per_device, mesh=mesh, in_specs=in_specs, out_specs=out_specs, check_vma=False
    )
```
